32 devices in a mesh: seq: 16 (over z, x, core), head: 2 (over y).
Axes of the slice: x: 2, y: 2, z: 4, core: 2. Of those that a mesh axis runs over, the one named last changes fastest.
Arguments:
- queries: bfloat16 [4096, 3072], P(('seq', 'head')), may hold values from -6 to 6
- keys: bfloat16 [4096, 3072], P('seq', 'head'), may hold values from -6 to 6
- values: bfloat16 [4096, 3072], P('seq', 'head'), may hold values from -6 to 6
- window: int32 [16, 27], P('seq'), may hold values from -1 to 15, as said below
- out_weight: bfloat16 [3072, 6144], P('seq', 'head'), may hold values from -0.109375 to 0.109375
Outputs:
- projected: bfloat16 [4096, 6144], P('seq', 'head')
The draws below stay inside these ranges and needn't reach their ends.
Inputs may be any that keep to these rules, and one draw needn't show every extreme that they name: Tile g lies at (g // 16, g // 4 % 4, g % 4) in a grid of 1 x 4 x 4 tiles. Entry k of window[g] is either -1 or the tile that lies (k // 9 - 1, k // 3 % 3 - 1, k % 3 - 1) steps away from g along time, height and width; it is -1 where that tile is outside the grid. Entry 13 is g itself.
All inputs are finite; a program needn't handle non-finite values.
Results may differ from the reference program's by a relative error of at most 0.0075.
Values may be sent and summed in bfloat16 or wider, within the bound.
No kernel may reach another device: no remote copies, remote signals or barrier semaphores. Data moves between devices by JAX's collectives and lax.ppermute only.
A program may use at most 64 MiB of HBM per device.

```python
import jax
import jax.numpy as jnp
from jax import lax

TILE = 256
HEADS = 24
HEAD_DIM = 128
D = 6144
GH = 4
GW = 4
SLOTS = 27
TILES = 16
GT = 1
TOKENS = 4096


def base_draw(key, stream_id):
    return jnp.clip(jax.random.normal(jax.random.fold_in(key, stream_id), (TOKENS, HEADS * HEAD_DIM)) * 1.5, -6.0, 6.0)


def draw_queries(key, part):
    drawn = base_draw(key, 11)
    return drawn.astype(jnp.bfloat16)


def draw_keys(key, part):
    drawn = base_draw(key, 21)
    return drawn.astype(jnp.bfloat16)


def draw_window(key, part):
    tile_ids = jnp.arange(TILES, dtype=jnp.int32)[:, None]
    slot_ids = jnp.arange(SLOTS, dtype=jnp.int32)[None, :]
    time_pos = tile_ids // (GH * GW)
    row_pos = tile_ids // GW % GH
    col_pos = tile_ids % GW
    time_step = slot_ids // 9 - 1
    row_step = slot_ids // 3 % 3 - 1
    col_step = slot_ids % 3 - 1
    new_time = time_pos + time_step
    new_row = row_pos + row_step
    new_col = col_pos + col_step
    inside = (new_time >= 0) & (new_time < GT) & (new_row >= 0) & (new_row < GH) & (new_col >= 0) & (new_col < GW)
    target = (new_time * GH + new_row) * GW + new_col
    percent = jax.random.randint(jax.random.fold_in(key, 31), (TILES, 1), 30, 101)
    rolled = jax.random.randint(jax.random.fold_in(key, 32), (TILES, SLOTS), 0, 100)
    kept = inside & ((rolled < percent) | (slot_ids == 13))
    return jnp.where(kept, target, -1).astype(jnp.int32)


def steps_of(own_key, dims, cuts, low, largest):
    def one(dim, blocks):
        heights = jax.random.uniform(jax.random.fold_in(jax.random.fold_in(own_key, 6), dim), (blocks,), jnp.float32, low / len(cuts), largest / len(cuts))
        return jnp.repeat(jnp.exp(heights), dims[dim] // blocks).reshape((-1,) + (1,) * (len(dims) - dim - 1))

    factor_of = one(*cuts[0])
    for cut in cuts[1:]:
        factor_of = factor_of * one(*cut)
    return factor_of


def bell_draw(own_key, dims, scale, reach, split=(), held_as=jnp.bfloat16):
    values = scale * jax.random.normal(own_key, dims, jnp.float32)
    if split:
        values = values * steps_of(own_key, dims, split, -0.22, 0.18)
    return jnp.clip(values, -reach, reach).astype(held_as)


def setup_inputs(seed: int = 0) -> dict:
    arg_keys = jax.random.split(jax.random.key(seed), 6)
    queries = draw_queries(jax.random.fold_in(arg_keys[5], 71), 0)
    keys = draw_keys(jax.random.fold_in(arg_keys[5], 71), 0)
    values = bell_draw(arg_keys[2], (TOKENS, HEADS * HEAD_DIM), 1.0, 6.0, ((0, 16), (1, 2)))
    window = draw_window(jax.random.fold_in(arg_keys[5], 71), 0)
    out_weight = bell_draw(arg_keys[4], (HEADS * HEAD_DIM, D), (HEADS * HEAD_DIM) ** -0.5, 0.109375, ((0, 16), (1, 2)))
    return dict(queries=queries, keys=keys, values=values, window=window, out_weight=out_weight)


def reference(queries, keys, values, window, out_weight):
    tile_count = TOKENS // TILE
    tiled = (tile_count, TILE, HEADS, HEAD_DIM)
    query_tiles = queries.reshape(tiled)
    key_tiles = keys.reshape(tiled)
    value_tiles = values.reshape(tiled)
    factor = HEAD_DIM ** -0.5

    def one_tile(tile_item):
        query_block, listed = tile_item
        listed_ok = listed >= 0
        clamped = jnp.where(listed_ok, listed, 0).astype(jnp.int32)
        key_block = key_tiles[clamped].reshape(SLOTS * TILE, HEADS, HEAD_DIM).astype(jnp.float32)
        value_block = value_tiles[clamped].reshape(SLOTS * TILE, HEADS, HEAD_DIM).astype(jnp.float32)
        scores = jnp.einsum("qhd,khd->qhk", query_block.astype(jnp.float32), key_block) * factor
        key_ok = jnp.repeat(listed_ok, TILE)[None, None, :]
        scores = jnp.where(key_ok, scores, -jnp.inf)
        row_max = jnp.max(scores, axis=-1, keepdims=True)
        weights = jnp.exp(scores - row_max)
        denominator = jnp.sum(weights, axis=-1)
        rounded = lax.optimization_barrier(weights.astype(jnp.bfloat16)).astype(jnp.float32)
        numerator = jnp.einsum("qhk,khd->qhd", rounded, value_block)
        return (numerator / denominator[:, :, None]).astype(jnp.bfloat16)

    attended = lax.map(one_tile, (query_tiles, window))
    attended = attended.reshape(TOKENS, HEADS * HEAD_DIM)
    return jnp.dot(attended, out_weight, preferred_element_type=jnp.float32).astype(jnp.bfloat16)
```

```python
import functools

import jax
import jax.numpy as jnp
from jax import lax
from jax.experimental import pallas as pl
from jax.experimental.pallas import tpu as pltpu
from jax.sharding import PartitionSpec as P

HEAD_DIM = 128
GH = 4
GW = 4
LOG2E = 1.4426950408889634
DEAD = -1e30


def passed_along(array, axis, by):
    count = lax.axis_size(axis)
    pairs = [(i, i + by) for i in range(count) if 0 <= i + by < count]
    return lax.ppermute(array, axis, pairs)


def attend_block(softmax_state, queries, kv_block, live_keys):
    run_max, run_sum, run_acc = softmax_state
    factor = queries.shape[-1] ** (-0.5)
    scores = (
        jnp.einsum("qhd,khd->qhk", queries, kv_block[0], preferred_element_type=jnp.float32)
        * factor
    )
    scores = jnp.where(live_keys[None, None, :], scores, -1e30)
    new_max = jnp.maximum(run_max, jnp.max(scores, axis=-1))
    rescale = jnp.exp(run_max - new_max)
    weights = jnp.where(live_keys[None, None, :], jnp.exp(scores - new_max[:, :, None]), 0.0)
    run_sum = run_sum * rescale + jnp.sum(weights, axis=-1)
    run_acc = run_acc * rescale[:, :, None] + jnp.einsum(
        "qhk,khd->qhd",
        weights.astype(jnp.bfloat16),
        kv_block[1],
        preferred_element_type=jnp.float32,
    )
    return (new_max, run_sum, run_acc)


def local_general(queries, keys, values, window, out_weight):
    tok_rows = queries.shape[0]
    head_width = HEAD_DIM
    heads_all = queries.shape[1] // head_width
    local_q = lax.all_to_all(
        queries.reshape(tok_rows, heads_all, head_width),
        "head",
        split_axis=1,
        concat_axis=0,
        tiled=True,
    )
    tile_rows = local_q.shape[0]
    heads_dev = local_q.shape[1]
    live_tiles = window[0] >= 0
    kv_pair = jnp.stack(
        [
            keys.reshape(tile_rows, heads_dev, head_width),
            values.reshape(tile_rows, heads_dev, head_width),
        ]
    )
    softmax_state = (
        jnp.full((tile_rows, heads_dev), -1e30, jnp.float32),
        jnp.zeros((tile_rows, heads_dev), jnp.float32),
        jnp.zeros((tile_rows, heads_dev, head_width), jnp.float32),
    )
    seq_span = lax.axis_size("seq")
    plane_size = GH * GW

    def tile_mask(first_slot, tile_count):
        return jnp.repeat(live_tiles[first_slot : first_slot + tile_count], tile_rows)

    from_left = passed_along(kv_pair, "seq", 1)
    from_right = passed_along(kv_pair, "seq", -1)
    kv_line = jnp.concatenate([from_left, kv_pair, from_right], axis=1)
    above = passed_along(kv_line, "seq", GW)
    below = passed_along(kv_line, "seq", -GW)
    kv_plane = jnp.concatenate([above, kv_line, below], axis=1)
    line_rows = 3 * tile_rows
    for row_index in (1, 0, 2):
        softmax_state = attend_block(
            softmax_state,
            local_q,
            kv_plane[:, row_index * line_rows : (row_index + 1) * line_rows],
            tile_mask(9 + 3 * row_index, 3),
        )
    if plane_size < seq_span:
        for depth_step in (-1, 1):
            kv_depth = passed_along(kv_plane, "seq", -depth_step * plane_size)
            for row_index in range(3):
                softmax_state = attend_block(
                    softmax_state,
                    local_q,
                    kv_depth[:, row_index * line_rows : (row_index + 1) * line_rows],
                    tile_mask(9 * (depth_step + 1) + 3 * row_index, 3),
                )
    run_max, run_sum, run_acc = softmax_state
    finished = (run_acc / run_sum[:, :, None]).astype(jnp.bfloat16)
    finished = finished.reshape(tile_rows, heads_dev * head_width)
    all_heads = lax.all_gather(finished, "head", axis=1, tiled=True)
    projected = jnp.dot(
        all_heads,
        lax.all_gather(out_weight, "seq", axis=0, tiled=True),
        preferred_element_type=jnp.float32,
    )
    return projected.astype(jnp.bfloat16)


def attend_kernel(tile, win, q_ref, own_ref, up_ref, dn_ref, o_ref, vt_ref):
    coef = q_ref.shape[1] ** -0.5 * LOG2E
    refs = (up_ref, own_ref, dn_ref)
    for r in range(3):
        for c in range(GW):
            vt_ref[r, :, c * tile : (c + 1) * tile] = refs[r][(2 * c + 1) * tile : (2 * c + 2) * tile, :].T
    for c in range(GW):
        q = q_ref[c * tile : (c + 1) * tile, :]
        lo, hi = max(c - 1, 0), min(c + 2, GW)
        top = total = acc = None
        for r in (1, 0, 2):
            scores, lives = [], []
            new = top
            for k in range(lo, hi):
                keys = refs[r][2 * k * tile : (2 * k + 1) * tile, :]
                s = lax.dot_general(keys, q, (((1,), (1,)), ((), ())), preferred_element_type=jnp.float32)
                live = win[c, 9 + 3 * r + k - c + 1] >= 0
                scores.append(s)
                lives.append(live)
                high = jnp.where(live, jnp.max(s, axis=0, keepdims=True), DEAD)
                new = high if new is None else jnp.maximum(new, high)
            weights, part = [], None
            for s, live in zip(scores, lives):
                w = jnp.exp2((s - jnp.where(live, new, -DEAD)) * coef)
                w_sum = jnp.sum(w, axis=0, keepdims=True)
                part = w_sum if part is None else part + w_sum
                weights.append(w.astype(jnp.bfloat16))
            pv = jnp.dot(
                vt_ref[r, :, lo * tile : hi * tile],
                jnp.concatenate(weights, axis=0),
                preferred_element_type=jnp.float32,
            )
            if top is None:
                total, acc = part, pv
            else:
                again = jnp.exp2((top - new) * coef)
                total = total * again + part
                acc = acc * again + pv
            top = new
        o_ref[c * tile : (c + 1) * tile, :] = (acc / total).astype(jnp.bfloat16).T


def attend_line(win, q, own, up, dn):
    rows, width = q.shape
    tile = rows // GW
    units = 3 * (3 * GW - 2)
    return pl.pallas_call(
        functools.partial(attend_kernel, tile),
        out_shape=jax.ShapeDtypeStruct(q.shape, jnp.bfloat16),
        in_specs=[pl.BlockSpec(memory_space=pltpu.SMEM)] + [pl.BlockSpec(memory_space=pltpu.VMEM)] * 4,
        out_specs=pl.BlockSpec(memory_space=pltpu.VMEM),
        scratch_shapes=[pltpu.VMEM((3, width, rows), jnp.bfloat16)],
        compiler_params=pltpu.CompilerParams(vmem_limit_bytes=40 * 2**20),
        cost_estimate=pl.CostEstimate(
            flops=units * 4 * tile * tile * width,
            bytes_accessed=16 * rows * width,
            transcendentals=units * tile * tile,
        ),
    )(win, q, own, up, dn)


def project_kernel(steps, width, place, *refs):
    pieces, w_ref, o_ref = refs[:-2], refs[-2], refs[-1]
    acc = None
    for i in range(0, len(pieces), 2):
        left = jnp.concatenate([pieces[i][...], pieces[i + 1][...]], axis=1)
        right = jnp.concatenate(
            [w_ref[pl.ds(pl.multiple_of(place[i + j], width), width), :] for j in (0, 1)], axis=0
        )
        d = jnp.dot(left, right, preferred_element_type=jnp.float32)
        acc = d if acc is None else acc + d
    o_ref[...] = acc.astype(jnp.bfloat16)


def project(place, pieces, w):
    rows, width = pieces[0].shape
    step = rows // GW
    return pl.pallas_call(
        functools.partial(project_kernel, GW, width),
        out_shape=jax.ShapeDtypeStruct((rows, w.shape[1]), jnp.bfloat16),
        grid_spec=pltpu.PrefetchScalarGridSpec(
            num_scalar_prefetch=1,
            grid=(GW,),
            in_specs=[pl.BlockSpec((step, width), lambda i, place: (i, 0))] * len(pieces)
            + [pl.BlockSpec(w.shape, lambda i, place: (0, 0))],
            out_specs=pl.BlockSpec((step, w.shape[1]), lambda i, place: (i, 0)),
        ),
        compiler_params=pltpu.CompilerParams(vmem_limit_bytes=40 * 2**20),
        cost_estimate=pl.CostEstimate(
            flops=2 * rows * w.shape[0] * w.shape[1],
            bytes_accessed=2 * (rows * w.shape[0] + w.shape[0] * w.shape[1] + rows * w.shape[1]),
            transcendentals=0,
        ),
    )(place, *pieces, w)


def local_plane(queries, keys, values, window, out_weight):
    span = lax.axis_size("seq")
    lines = [[r + c for c in range(GW)] for r in range(0, span, GW)]
    columns = [[r + c for r in range(0, span, GW)] for c in range(GW)]
    down = [(i, i + GW) for i in range(span - GW)]
    up = [(i + GW, i) for i in range(span - GW)]
    own_width = keys.shape[1]
    width = HEAD_DIM
    steps = own_width // (GW * width)
    part = GW * width
    chunks = out_weight.shape[1] // (GW * 256)
    cut = out_weight.shape[1] // chunks

    def over_line(array, split, concat):
        return lax.all_to_all(array, "seq", split, concat, axis_index_groups=lines, tiled=True)

    def swap(array, by):
        return lax.ppermute(array, "seq", [(i, i ^ by) for i in range(span)])

    win = lax.all_gather(window, "seq", axis=0, tiled=True, axis_index_groups=lines)
    w_own = [over_line(out_weight[:, n * cut : (n + 1) * cut], 1, 0) for n in range(chunks)]
    w_all = [lax.all_gather(w, "seq", axis=0, tiled=True, axis_index_groups=columns) for w in w_own]

    q = lax.all_to_all(queries, "head", 1, 0, tiled=True)
    pieces, homes = [], []
    for h in range(steps):
        cols = slice(h * part, (h + 1) * part)
        kv = over_line(jnp.concatenate([keys[:, cols], values[:, cols]], axis=0), 1, 0)
        kv_up = lax.ppermute(kv, "seq", down)
        kv_dn = lax.ppermute(kv, "seq", up)
        mine = attend_line(win, over_line(q[:, cols], 1, 0), kv, kv_up, kv_dn)
        held = [(mine, 0, 0), (lax.ppermute(mine, "head", [(0, 1), (1, 0)]), 1, 0)]
        held += [(swap(a, 2), y, c + 2) for a, y, c in held]
        held += [(swap(a, 1), y, c + 1) for a, y, c in held]
        pieces += [a for a, _, _ in held]
        homes += [(y, c, h) for _, y, c in held]

    y_own = lax.axis_index("head")
    c_own = lax.axis_index("seq") % GW
    homes = jnp.asarray(homes, jnp.int32)
    place = (homes[:, 0] ^ y_own) * own_width + homes[:, 2] * part + (homes[:, 1] ^ c_own) * width
    outs = [over_line(project(place, pieces, w), 0, 1) for w in w_all]
    return jnp.concatenate(outs, axis=1)


def solution(mesh):
    span, sides = mesh.shape["seq"], mesh.shape["head"]

    def local(queries, keys, values, window, out_weight):
        one_step = span == GH * GW and sides == 2
        even = keys.shape[1] % (GW * HEAD_DIM) == 0 and out_weight.shape[1] % (GW * 256) == 0
        which = local_plane if one_step and even else local_general
        return which(queries, keys, values, window, out_weight)

    in_specs = (
        P(("seq", "head"), None),
        P("seq", "head"),
        P("seq", "head"),
        P("seq", None),
        P("seq", "head"),
    )
    out_specs = P("seq", "head")
    return jax.shard_map(local, mesh=mesh, in_specs=in_specs, out_specs=out_specs, check_vma=False)
```

```python
import functools

import jax
import jax.numpy as jnp
from jax import lax
from jax.experimental import pallas as pl
from jax.experimental.pallas import tpu as pltpu
from jax.sharding import PartitionSpec as P

HEAD_DIM = 128
GH = 4
GW = 4
LOG2E = 1.4426950408889634
DEAD = -1e30


def passed_along(array, axis, by):
    count = lax.axis_size(axis)
    pairs = [(i, i + by) for i in range(count) if 0 <= i + by < count]
    return lax.ppermute(array, axis, pairs)


def attend_block(softmax_state, queries, kv_block, live_keys):
    run_max, run_sum, run_acc = softmax_state
    factor = queries.shape[-1] ** (-0.5)
    scores = (
        jnp.einsum("qhd,khd->qhk", queries, kv_block[0], preferred_element_type=jnp.float32)
        * factor
    )
    scores = jnp.where(live_keys[None, None, :], scores, -1e30)
    new_max = jnp.maximum(run_max, jnp.max(scores, axis=-1))
    rescale = jnp.exp(run_max - new_max)
    weights = jnp.where(live_keys[None, None, :], jnp.exp(scores - new_max[:, :, None]), 0.0)
    run_sum = run_sum * rescale + jnp.sum(weights, axis=-1)
    run_acc = run_acc * rescale[:, :, None] + jnp.einsum(
        "qhk,khd->qhd",
        weights.astype(jnp.bfloat16),
        kv_block[1],
        preferred_element_type=jnp.float32,
    )
    return (new_max, run_sum, run_acc)


def local_general(queries, keys, values, window, out_weight):
    tok_rows = queries.shape[0]
    head_width = HEAD_DIM
    heads_all = queries.shape[1] // head_width
    local_q = lax.all_to_all(
        queries.reshape(tok_rows, heads_all, head_width),
        "head",
        split_axis=1,
        concat_axis=0,
        tiled=True,
    )
    tile_rows = local_q.shape[0]
    heads_dev = local_q.shape[1]
    live_tiles = window[0] >= 0
    kv_pair = jnp.stack(
        [
            keys.reshape(tile_rows, heads_dev, head_width),
            values.reshape(tile_rows, heads_dev, head_width),
        ]
    )
    softmax_state = (
        jnp.full((tile_rows, heads_dev), -1e30, jnp.float32),
        jnp.zeros((tile_rows, heads_dev), jnp.float32),
        jnp.zeros((tile_rows, heads_dev, head_width), jnp.float32),
    )
    seq_span = lax.axis_size("seq")
    plane_size = GH * GW

    def tile_mask(first_slot, tile_count):
        return jnp.repeat(live_tiles[first_slot : first_slot + tile_count], tile_rows)

    from_left = passed_along(kv_pair, "seq", 1)
    from_right = passed_along(kv_pair, "seq", -1)
    kv_line = jnp.concatenate([from_left, kv_pair, from_right], axis=1)
    above = passed_along(kv_line, "seq", GW)
    below = passed_along(kv_line, "seq", -GW)
    kv_plane = jnp.concatenate([above, kv_line, below], axis=1)
    line_rows = 3 * tile_rows
    for row_index in (1, 0, 2):
        softmax_state = attend_block(
            softmax_state,
            local_q,
            kv_plane[:, row_index * line_rows : (row_index + 1) * line_rows],
            tile_mask(9 + 3 * row_index, 3),
        )
    if plane_size < seq_span:
        for depth_step in (-1, 1):
            kv_depth = passed_along(kv_plane, "seq", -depth_step * plane_size)
            for row_index in range(3):
                softmax_state = attend_block(
                    softmax_state,
                    local_q,
                    kv_depth[:, row_index * line_rows : (row_index + 1) * line_rows],
                    tile_mask(9 * (depth_step + 1) + 3 * row_index, 3),
                )
    run_max, run_sum, run_acc = softmax_state
    finished = (run_acc / run_sum[:, :, None]).astype(jnp.bfloat16)
    finished = finished.reshape(tile_rows, heads_dev * head_width)
    all_heads = lax.all_gather(finished, "head", axis=1, tiled=True)
    projected = jnp.dot(
        all_heads,
        lax.all_gather(out_weight, "seq", axis=0, tiled=True),
        preferred_element_type=jnp.float32,
    )
    return projected.astype(jnp.bfloat16)


VMEM_LIMIT = 56 * 2**20


def attend_kernel(listed, q_ref, *refs):
    tiles, o_ref = refs[:9], refs[9]
    tile, width = q_ref.shape
    coef = width**-0.5 * LOG2E
    toward = 1 - 2 * (listed[27] & 1)
    q = q_ref[...]
    top = total = acc = None
    for r in (1, 0, 2):
        scores, lives = [], []
        new = top
        for k, step in enumerate((0, toward, -toward)):
            s = lax.dot_general(
                tiles[3 * r + k][:tile, :], q, (((1,), (1,)), ((), ())), preferred_element_type=jnp.float32
            )
            live = listed[10 + 3 * r + step] >= 0
            scores.append(s)
            lives.append(live)
            high = jnp.where(live, jnp.max(s, axis=0, keepdims=True), DEAD)
            new = high if new is None else jnp.maximum(new, high)
        weights, part = [], None
        for s, live in zip(scores, lives):
            w = jnp.exp2((s - jnp.where(live, new, -DEAD)) * coef)
            w_sum = jnp.sum(w, axis=0, keepdims=True)
            part = w_sum if part is None else part + w_sum
            weights.append(w.astype(jnp.bfloat16))
        values = jnp.concatenate([tiles[3 * r + k][tile:, :].T for k in range(3)], axis=1)
        pv = jnp.dot(values, jnp.concatenate(weights, axis=0), preferred_element_type=jnp.float32)
        if top is None:
            total, acc = part, pv
        else:
            again = jnp.exp2((top - new) * coef)
            total = total * again + part
            acc = acc * again + pv
        top = new
    o_ref[...] = (acc / total).astype(jnp.bfloat16).T


def attend_tile(listed, q, first, tiles):
    rows = q.shape[0]
    heads = tiles[0].shape[1] // HEAD_DIM
    return pl.pallas_call(
        attend_kernel,
        out_shape=jax.ShapeDtypeStruct((rows, heads * HEAD_DIM), jnp.bfloat16),
        grid_spec=pltpu.PrefetchScalarGridSpec(
            num_scalar_prefetch=1,
            grid=(heads,),
            in_specs=[pl.BlockSpec((rows, HEAD_DIM), lambda h, listed: (0, first + h))]
            + [pl.BlockSpec((2 * rows, HEAD_DIM), lambda h, listed: (0, h))] * len(tiles),
            out_specs=pl.BlockSpec((rows, HEAD_DIM), lambda h, listed: (0, h)),
        ),
        compiler_params=pltpu.CompilerParams(vmem_limit_bytes=VMEM_LIMIT),
        cost_estimate=pl.CostEstimate(
            flops=heads * 36 * rows * rows * HEAD_DIM,
            bytes_accessed=40 * heads * rows * HEAD_DIM,
            transcendentals=heads * 9 * rows * rows,
        ),
    )(listed, q, *tiles)


def local_plane(queries, keys, values, window, out_weight):
    span = lax.axis_size("seq")
    down = [(i, i + GW) for i in range(span - GW)]
    up = [(i + GW, i) for i in range(span - GW)]
    mates = [(i, i ^ 1) for i in range(span)]
    outer = [(i, i ^ 3) for i in range(span) if i % GW in (1, 2)]
    side = lax.axis_index("head")

    def move(array, pairs):
        return lax.ppermute(array, "seq", pairs)

    parts = 1
    wide = out_weight.shape[1] // parts
    w_all = [
        lax.all_gather(out_weight[:, n * wide : (n + 1) * wide], "seq", axis=0, tiled=True) for n in range(parts)
    ]

    chunk = keys.shape[1] // 2
    listed = jnp.concatenate([window[0], lax.axis_index("seq")[None]])
    held = []
    for at in (0, chunk):
        kv = jnp.concatenate([keys[:, at : at + chunk], values[:, at : at + chunk]], axis=0)
        kv_out = move(kv, outer)
        kv_up, kv_dn = move(kv, down), move(kv, up)
        out_up = move(kv_out, [p for p in down if p[0] % GW in (1, 2)])
        out_dn = move(kv_out, [p for p in up if p[0] % GW in (1, 2)])
        held.append([kv_up, move(kv_up, mates), out_up, kv, move(kv, mates), kv_out, kv_dn, move(kv_dn, mates), out_dn])

    q = lax.all_to_all(queries, "head", 1, 0, tiled=True)
    mine = [attend_tile(listed, q, n * chunk // HEAD_DIM, tiles) for n, tiles in enumerate(held)]
    other = [lax.ppermute(a, "head", [(0, 1), (1, 0)]) for a in mine]
    attended = jnp.where(side == 0, jnp.concatenate(mine + other, axis=1), jnp.concatenate(other + mine, axis=1))
    made = [jnp.dot(attended, w, preferred_element_type=jnp.float32).astype(jnp.bfloat16) for w in w_all]
    return jnp.concatenate(made, axis=1)


def solution(mesh):
    span, sides = mesh.shape["seq"], mesh.shape["head"]

    def local(queries, keys, values, window, out_weight):
        one_step = span == GH * GW and sides == 2
        even = keys.shape[1] % (2 * HEAD_DIM) == 0
        which = local_plane if one_step and even else local_general
        return which(queries, keys, values, window, out_weight)

    in_specs = (
        P(("seq", "head"), None),
        P("seq", "head"),
        P("seq", "head"),
        P("seq", None),
        P("seq", "head"),
    )
    out_specs = P("seq", "head")
    return jax.shard_map(local, mesh=mesh, in_specs=in_specs, out_specs=out_specs, check_vma=False)
```

```python
import functools

import jax
import jax.numpy as jnp
from jax import lax
from jax.experimental import pallas as pl
from jax.experimental.pallas import tpu as pltpu
from jax.sharding import PartitionSpec as P

HEAD_DIM = 128
GH = 4
GW = 4
LOG2E = 1.4426950408889634
DEAD = -1e30


def passed_along(array, axis, by):
    count = lax.axis_size(axis)
    pairs = [(i, i + by) for i in range(count) if 0 <= i + by < count]
    return lax.ppermute(array, axis, pairs)


def attend_block(softmax_state, queries, kv_block, live_keys):
    run_max, run_sum, run_acc = softmax_state
    factor = queries.shape[-1] ** (-0.5)
    scores = (
        jnp.einsum("qhd,khd->qhk", queries, kv_block[0], preferred_element_type=jnp.float32)
        * factor
    )
    scores = jnp.where(live_keys[None, None, :], scores, -1e30)
    new_max = jnp.maximum(run_max, jnp.max(scores, axis=-1))
    rescale = jnp.exp(run_max - new_max)
    weights = jnp.where(live_keys[None, None, :], jnp.exp(scores - new_max[:, :, None]), 0.0)
    run_sum = run_sum * rescale + jnp.sum(weights, axis=-1)
    run_acc = run_acc * rescale[:, :, None] + jnp.einsum(
        "qhk,khd->qhd",
        weights.astype(jnp.bfloat16),
        kv_block[1],
        preferred_element_type=jnp.float32,
    )
    return (new_max, run_sum, run_acc)


def local_general(queries, keys, values, window, out_weight):
    tok_rows = queries.shape[0]
    head_width = HEAD_DIM
    heads_all = queries.shape[1] // head_width
    local_q = lax.all_to_all(
        queries.reshape(tok_rows, heads_all, head_width),
        "head",
        split_axis=1,
        concat_axis=0,
        tiled=True,
    )
    tile_rows = local_q.shape[0]
    heads_dev = local_q.shape[1]
    live_tiles = window[0] >= 0
    kv_pair = jnp.stack(
        [
            keys.reshape(tile_rows, heads_dev, head_width),
            values.reshape(tile_rows, heads_dev, head_width),
        ]
    )
    softmax_state = (
        jnp.full((tile_rows, heads_dev), -1e30, jnp.float32),
        jnp.zeros((tile_rows, heads_dev), jnp.float32),
        jnp.zeros((tile_rows, heads_dev, head_width), jnp.float32),
    )
    seq_span = lax.axis_size("seq")
    plane_size = GH * GW

    def tile_mask(first_slot, tile_count):
        return jnp.repeat(live_tiles[first_slot : first_slot + tile_count], tile_rows)

    from_left = passed_along(kv_pair, "seq", 1)
    from_right = passed_along(kv_pair, "seq", -1)
    kv_line = jnp.concatenate([from_left, kv_pair, from_right], axis=1)
    above = passed_along(kv_line, "seq", GW)
    below = passed_along(kv_line, "seq", -GW)
    kv_plane = jnp.concatenate([above, kv_line, below], axis=1)
    line_rows = 3 * tile_rows
    for row_index in (1, 0, 2):
        softmax_state = attend_block(
            softmax_state,
            local_q,
            kv_plane[:, row_index * line_rows : (row_index + 1) * line_rows],
            tile_mask(9 + 3 * row_index, 3),
        )
    if plane_size < seq_span:
        for depth_step in (-1, 1):
            kv_depth = passed_along(kv_plane, "seq", -depth_step * plane_size)
            for row_index in range(3):
                softmax_state = attend_block(
                    softmax_state,
                    local_q,
                    kv_depth[:, row_index * line_rows : (row_index + 1) * line_rows],
                    tile_mask(9 * (depth_step + 1) + 3 * row_index, 3),
                )
    run_max, run_sum, run_acc = softmax_state
    finished = (run_acc / run_sum[:, :, None]).astype(jnp.bfloat16)
    finished = finished.reshape(tile_rows, heads_dev * head_width)
    all_heads = lax.all_gather(finished, "head", axis=1, tiled=True)
    projected = jnp.dot(
        all_heads,
        lax.all_gather(out_weight, "seq", axis=0, tiled=True),
        preferred_element_type=jnp.float32,
    )
    return projected.astype(jnp.bfloat16)


VMEM_LIMIT = 56 * 2**20


def attend_kernel(listed, q_ref, *refs):
    keys, values, o_ref = refs[:9], refs[9:18], refs[-1]
    coef = q_ref.shape[1] ** -0.5 * LOG2E
    toward = 1 - 2 * (listed[27] & 1)
    q = q_ref[...]
    top = total = acc = None
    for r in (1, 0, 2):
        scores, lives = [], []
        new = top
        for k, step in enumerate((0, toward, -toward)):
            s = lax.dot_general(
                keys[3 * r + k][...], q, (((1,), (1,)), ((), ())), preferred_element_type=jnp.float32
            )
            live = listed[10 + 3 * r + step] >= 0
            scores.append(s)
            lives.append(live)
            high = jnp.where(live, jnp.max(s, axis=0, keepdims=True), DEAD)
            new = high if new is None else jnp.maximum(new, high)
        weights, part = [], None
        for s, live in zip(scores, lives):
            w = jnp.exp2((s - jnp.where(live, new, -DEAD)) * coef)
            w_sum = jnp.sum(w, axis=0, keepdims=True)
            part = w_sum if part is None else part + w_sum
            weights.append(w.astype(jnp.bfloat16))
        sides = jnp.concatenate([values[3 * r + k][...].T for k in range(3)], axis=1)
        pv = jnp.dot(sides, jnp.concatenate(weights, axis=0), preferred_element_type=jnp.float32)
        if top is None:
            total, acc = part, pv
        else:
            again = jnp.exp2((top - new) * coef)
            total = total * again + part
            acc = acc * again + pv
        top = new
    o_ref[...] = (acc / total).astype(jnp.bfloat16).T


def attend_tile(listed, q, head, count, first, own, rows, before):
    tile = q.shape[0]

    def spec(block, at=first):
        return pl.BlockSpec((tile, HEAD_DIM), lambda h, listed: (block, at + h))

    return pl.pallas_call(
        attend_kernel,
        out_shape=jax.ShapeDtypeStruct((tile, count * HEAD_DIM), jnp.bfloat16),
        grid_spec=pltpu.PrefetchScalarGridSpec(
            num_scalar_prefetch=1,
            grid=(count,),
            in_specs=[spec(0, head)]
            + [spec(0)] * 3
            + [spec(0, head)] * 3
            + [spec(2)] * 3
            + [spec(1)] * 3
            + [spec(1, head)] * 3
            + [spec(3)] * 3
            + [pl.BlockSpec(memory_space=pl.ANY)] * len(before),
            out_specs=pl.BlockSpec((tile, HEAD_DIM), lambda h, listed: (0, h)),
        ),
        compiler_params=pltpu.CompilerParams(vmem_limit_bytes=VMEM_LIMIT),
        cost_estimate=pl.CostEstimate(
            flops=count * 36 * tile * tile * HEAD_DIM,
            bytes_accessed=40 * count * tile * HEAD_DIM,
            transcendentals=count * 9 * tile * tile,
        ),
    )(listed, q, *rows, *own, *rows, *rows, *own, *rows, *before)


def project_kernel(planes, wides, spot, *refs):
    count = 4 * len(wides)
    pieces, refs = refs[:count], refs[count:]
    if wides:
        w_hbm, here, there, a_ref, w_ref, acc, sems = refs
    else:
        a_ref, w_hbm, here, there, w_ref, acc, sems = refs
    outs = (here, there)
    tile = a_ref.shape[0] // 2
    shard = w_ref.shape[0] // (planes * GW)
    block = GW * shard
    loads, copies, at = [], [], 0
    for n, wide in enumerate(wides):
        for i in range(4):
            col = (spot[0] if i < 2 else 1 - spot[0]) * sum(wides) + at
            dst = a_ref.at[pl.ds(i % 2 * tile, tile), pl.ds(pl.multiple_of(col, 128), wide)]
            loads.append(pltpu.make_async_copy(pieces[4 * n + i], dst, sems.at[4 * n + i]))
        at += wide
    for z in range(planes):
        for c in range(GW):
            src = w_hbm.at[pl.ds((z * GW + c % 2 * 2 + c // 2) * shard, shard), :]
            dst = w_ref.at[pl.ds((z * GW + c) * shard, shard), :]
            copies.append(pltpu.make_async_copy(src, dst, sems.at[count + z * GW + c]))
    for c in loads + copies:
        c.start()
    for c in loads:
        c.wait()
    for z in range(planes):
        for c in copies[z * GW : (z + 1) * GW]:
            c.wait()
        d = jnp.dot(
            a_ref[:, z * block : (z + 1) * block],
            w_ref[z * block : (z + 1) * block, :],
            preferred_element_type=jnp.float32,
        )
        if z == 0:
            acc[...] = d
        elif z < planes - 1:
            acc[...] += d
        else:
            d = acc[...] + d
            for i in range(2):
                outs[i][...] = d[i * tile : (i + 1) * tile, :].astype(jnp.bfloat16)


def project(spot, pieces, w, planes, before):
    deep, cols = w.shape
    whole = len(pieces) == 1
    tile = pieces[0].shape[0] // (2 if whole else 1)
    wides = [] if whole else [p.shape[1] for p in pieces[::4]]
    vmem, hbm = pl.BlockSpec(memory_space=pltpu.VMEM), pl.BlockSpec(memory_space=pl.ANY)
    made = jax.ShapeDtypeStruct((tile, cols), jnp.bfloat16)
    put = jax.ShapeDtypeStruct((2 * tile, deep), jnp.bfloat16)
    outs = pl.pallas_call(
        lambda spot, *refs: project_kernel(
            planes, wides, spot, *refs[: len(pieces) + 1], *refs[len(pieces) + 1 + len(before) :]
        ),
        out_shape=[made, made] + ([] if whole else [put]),
        in_specs=[pl.BlockSpec(memory_space=pltpu.SMEM)]
        + [vmem if whole else hbm] * len(pieces)
        + [hbm] * (1 + len(before)),
        out_specs=[vmem] * (2 if whole else 3),
        scratch_shapes=[
            pltpu.VMEM((deep, cols), jnp.bfloat16),
            pltpu.VMEM((2 * tile, cols), jnp.float32),
            pltpu.SemaphoreType.DMA((4 * len(wides) + planes * GW,)),
        ],
        compiler_params=pltpu.CompilerParams(vmem_limit_bytes=VMEM_LIMIT),
        cost_estimate=pl.CostEstimate(
            flops=4 * tile * deep * cols,
            bytes_accessed=2 * (2 * tile * deep + deep * cols + 2 * tile * cols),
            transcendentals=0,
        ),
    )(spot, *pieces, w, *before)
    return [*outs, *(pieces if whole else [])]


def local_plane(queries, keys, values, window, out_weight):
    span = lax.axis_size("seq")
    planes = span // GW
    down = [(i, i + GW) for i in range(span - GW)]
    up = [(i + GW, i) for i in range(span - GW)]
    mates = [(i, i ^ 1) for i in range(span)]
    outer = [(i, i ^ 3) for i in range(span) if i % GW in (1, 2)]
    partners = [(i, i ^ 2) for i in range(span)]
    both_cores = [[z * GW + x * 2 + k for z in range(planes) for k in range(2)] for x in range(2)]
    seq, side = lax.axis_index("seq"), lax.axis_index("head")
    half = seq // 2 % 2
    tile, own_width = keys.shape
    heads = own_width // HEAD_DIM

    def move(array, pairs):
        return lax.ppermute(array, "seq", pairs)

    def in_order(flag, own, other, axis):
        return jnp.where(
            flag == 0, jnp.concatenate([own, other], axis=axis), jnp.concatenate([other, own], axis=axis)
        )

    def line(array):
        return [array, move(array, mates), move(array, outer)]

    kv = jnp.concatenate([keys, values], axis=0)
    kv_up, kv_dn = move(kv, down), move(kv, up)
    q = lax.all_to_all(queries, "head", 1, 0, tiled=True)

    cols = out_weight.shape[1] // 2
    w_mine = lax.dynamic_slice_in_dim(out_weight, half * cols, cols, 1)
    w_theirs = move(lax.dynamic_slice_in_dim(out_weight, (1 - half) * cols, cols, 1), partners)
    w_cuts = [0, cols * 2 // 3 // 256 * 256, cols]
    w_rows = [in_order(half, w_mine[:, lo:hi], w_theirs[:, lo:hi], 0) for lo, hi in zip(w_cuts[:-1], w_cuts[1:])]

    kv, w_rows = lax.optimization_barrier((kv, w_rows))
    own = line(kv)

    kv_up, kv_dn, own, q, w_rows = lax.optimization_barrier((kv_up, kv_dn, own, q, w_rows))
    w_all = [lax.all_gather(r, "seq", axis=0, tiled=True, axis_index_groups=both_cores) for r in w_rows]

    part = heads // 3
    cuts = [0, 2 * part * HEAD_DIM, own_width]
    rows = [
        line(jnp.concatenate([kv_up[:, lo:hi], kv_dn[:, lo:hi]], axis=0)) for lo, hi in zip(cuts[:-1], cuts[1:])
    ]

    listed = jnp.concatenate([window[0], seq[None]])
    pieces = []
    for n, (held, first) in enumerate(((0, 0), (0, part), (1, 0))):
        mine = attend_tile(listed, q, n * part, part, first, own, rows[held], pieces[1:4] if n == 2 else [])
        pieces += [
            mine,
            move(mine, partners),
            lax.ppermute(mine, "head", [(0, 1), (1, 0)]),
            lax.ppermute(mine, ("seq", "head"), [(2 * i + y, 2 * (i ^ 2) + 1 - y) for i in range(span) for y in (0, 1)]),
        ]

    spot = jnp.stack([side, half])
    own, other = [], []
    for w in w_all:
        here, there, *pieces = project(spot, pieces, w, planes, other)
        own.append(here)
        other.append(move(there, partners))
    done = in_order(half, jnp.concatenate(own, axis=1), jnp.pad(other[0], ((0, 0), (0, cols - w_cuts[1]))), 1)
    return lax.dynamic_update_slice(done, other[1], (0, (1 - half) * cols + w_cuts[1]))


def solution(mesh):
    span, sides = mesh.shape["seq"], mesh.shape["head"]

    def local(queries, keys, values, window, out_weight):
        one_step = span == GH * GW and sides == 2
        even = keys.shape[1] % (3 * HEAD_DIM) == 0 and out_weight.shape[1] % 1536 == 0
        which = local_plane if one_step and even else local_general
        return which(queries, keys, values, window, out_weight)

    in_specs = (
        P(("seq", "head"), None),
        P("seq", "head"),
        P("seq", "head"),
        P("seq", None),
        P("seq", "head"),
    )
    out_specs = P("seq", "head")
    return jax.shard_map(local, mesh=mesh, in_specs=in_specs, out_specs=out_specs, check_vma=False)
```

```python
import functools

import jax
import jax.numpy as jnp
from jax import lax
from jax.experimental import pallas as pl
from jax.experimental.pallas import tpu as pltpu
from jax.sharding import PartitionSpec as P

HEAD_DIM = 128
GH = 4
GW = 4
LOG2E = 1.4426950408889634
DEAD = -1e30


def passed_along(array, axis, by):
    count = lax.axis_size(axis)
    pairs = [(i, i + by) for i in range(count) if 0 <= i + by < count]
    return lax.ppermute(array, axis, pairs)


def attend_block(softmax_state, queries, kv_block, live_keys):
    run_max, run_sum, run_acc = softmax_state
    factor = queries.shape[-1] ** (-0.5)
    scores = (
        jnp.einsum("qhd,khd->qhk", queries, kv_block[0], preferred_element_type=jnp.float32)
        * factor
    )
    scores = jnp.where(live_keys[None, None, :], scores, -1e30)
    new_max = jnp.maximum(run_max, jnp.max(scores, axis=-1))
    rescale = jnp.exp(run_max - new_max)
    weights = jnp.where(live_keys[None, None, :], jnp.exp(scores - new_max[:, :, None]), 0.0)
    run_sum = run_sum * rescale + jnp.sum(weights, axis=-1)
    run_acc = run_acc * rescale[:, :, None] + jnp.einsum(
        "qhk,khd->qhd",
        weights.astype(jnp.bfloat16),
        kv_block[1],
        preferred_element_type=jnp.float32,
    )
    return (new_max, run_sum, run_acc)


def local_general(queries, keys, values, window, out_weight):
    tok_rows = queries.shape[0]
    head_width = HEAD_DIM
    heads_all = queries.shape[1] // head_width
    local_q = lax.all_to_all(
        queries.reshape(tok_rows, heads_all, head_width),
        "head",
        split_axis=1,
        concat_axis=0,
        tiled=True,
    )
    tile_rows = local_q.shape[0]
    heads_dev = local_q.shape[1]
    live_tiles = window[0] >= 0
    kv_pair = jnp.stack(
        [
            keys.reshape(tile_rows, heads_dev, head_width),
            values.reshape(tile_rows, heads_dev, head_width),
        ]
    )
    softmax_state = (
        jnp.full((tile_rows, heads_dev), -1e30, jnp.float32),
        jnp.zeros((tile_rows, heads_dev), jnp.float32),
        jnp.zeros((tile_rows, heads_dev, head_width), jnp.float32),
    )
    seq_span = lax.axis_size("seq")
    plane_size = GH * GW

    def tile_mask(first_slot, tile_count):
        return jnp.repeat(live_tiles[first_slot : first_slot + tile_count], tile_rows)

    from_left = passed_along(kv_pair, "seq", 1)
    from_right = passed_along(kv_pair, "seq", -1)
    kv_line = jnp.concatenate([from_left, kv_pair, from_right], axis=1)
    above = passed_along(kv_line, "seq", GW)
    below = passed_along(kv_line, "seq", -GW)
    kv_plane = jnp.concatenate([above, kv_line, below], axis=1)
    line_rows = 3 * tile_rows
    for row_index in (1, 0, 2):
        softmax_state = attend_block(
            softmax_state,
            local_q,
            kv_plane[:, row_index * line_rows : (row_index + 1) * line_rows],
            tile_mask(9 + 3 * row_index, 3),
        )
    if plane_size < seq_span:
        for depth_step in (-1, 1):
            kv_depth = passed_along(kv_plane, "seq", -depth_step * plane_size)
            for row_index in range(3):
                softmax_state = attend_block(
                    softmax_state,
                    local_q,
                    kv_depth[:, row_index * line_rows : (row_index + 1) * line_rows],
                    tile_mask(9 * (depth_step + 1) + 3 * row_index, 3),
                )
    run_max, run_sum, run_acc = softmax_state
    finished = (run_acc / run_sum[:, :, None]).astype(jnp.bfloat16)
    finished = finished.reshape(tile_rows, heads_dev * head_width)
    all_heads = lax.all_gather(finished, "head", axis=1, tiled=True)
    projected = jnp.dot(
        all_heads,
        lax.all_gather(out_weight, "seq", axis=0, tiled=True),
        preferred_element_type=jnp.float32,
    )
    return projected.astype(jnp.bfloat16)


VMEM_LIMIT = 56 * 2**20


def attend_kernel(listed, q_ref, *refs):
    o_ref = refs[-1]
    keys, values = refs[:9], refs[9:18]
    coef = HEAD_DIM**-0.5 * LOG2E
    toward = 1 - 2 * (listed[27] & 1)
    for head in range(q_ref.shape[1] // HEAD_DIM):
        at = slice(head * HEAD_DIM, (head + 1) * HEAD_DIM)
        q = q_ref[:, at]
        top = total = acc = None
        for r in (1, 0, 2):
            scores, lives = [], []
            new = top
            for k, step in enumerate((0, toward, -toward)):
                s = lax.dot_general(
                    keys[3 * r + k][:, at], q, (((1,), (1,)), ((), ())), preferred_element_type=jnp.float32
                )
                live = listed[10 + 3 * r + step] >= 0
                scores.append(s)
                lives.append(live)
                high = jnp.where(live, jnp.max(s, axis=0, keepdims=True), DEAD)
                new = high if new is None else jnp.maximum(new, high)
            weights, part = [], None
            for s, live in zip(scores, lives):
                w = jnp.exp2((s - jnp.where(live, new, -DEAD)) * coef)
                w_sum = jnp.sum(w, axis=0, keepdims=True)
                part = w_sum if part is None else part + w_sum
                weights.append(w.astype(jnp.bfloat16))
            sides = jnp.concatenate([values[3 * r + k][:, at].T for k in range(3)], axis=1)
            pv = jnp.dot(sides, jnp.concatenate(weights, axis=0), preferred_element_type=jnp.float32)
            if top is None:
                total, acc = part, pv
            else:
                again = jnp.exp2((top - new) * coef)
                total = total * again + part
                acc = acc * again + pv
            top = new
        o_ref[:, at] = (acc / total).astype(jnp.bfloat16).T


AT_ONCE = 2


def attend_tile(listed, q, head, count, first, own, rows, before):
    tile = q.shape[0]

    def spec(block, at=first):
        return pl.BlockSpec((tile, AT_ONCE * HEAD_DIM), lambda h, listed: (block, at // AT_ONCE + h))

    return pl.pallas_call(
        attend_kernel,
        out_shape=jax.ShapeDtypeStruct((tile, count * HEAD_DIM), jnp.bfloat16),
        grid_spec=pltpu.PrefetchScalarGridSpec(
            num_scalar_prefetch=1,
            grid=(count // AT_ONCE,),
            in_specs=[spec(0, head)]
            + [spec(0)] * 3
            + [spec(0, head)] * 3
            + [spec(2)] * 3
            + [spec(1)] * 3
            + [spec(1, head)] * 3
            + [spec(3)] * 3
            + [pl.BlockSpec(memory_space=pl.ANY)] * len(before),
            out_specs=pl.BlockSpec((tile, AT_ONCE * HEAD_DIM), lambda h, listed: (0, h)),
        ),
        compiler_params=pltpu.CompilerParams(vmem_limit_bytes=VMEM_LIMIT),
        cost_estimate=pl.CostEstimate(flops=1, bytes_accessed=1, transcendentals=0),
    )(listed, q, *rows, *own, *rows, *rows, *own, *rows, *before)


def gather_kernel(spot, *refs):
    pieces, a_ref, sems = refs[:-2], refs[-2], refs[-1]
    tile = a_ref.shape[0] // 2
    side_width = a_ref.shape[1] // 2
    copies, at = [], 0
    for i, piece in enumerate(pieces):
        wide = piece.shape[1]
        col = (spot[0] if i % 4 < 2 else 1 - spot[0]) * side_width + at
        dst = a_ref.at[pl.ds(i % 2 * tile, tile), pl.ds(pl.multiple_of(col, 128), wide)]
        copies.append(pltpu.make_async_copy(piece, dst, sems.at[i]))
        at += wide if i % 4 == 3 else 0
    for c in copies:
        c.start()
    for c in copies:
        c.wait()


def gather_heads(spot, pieces):
    rows, width = 2 * pieces[0].shape[0], 2 * sum(p.shape[1] for p in pieces[::4])
    return pl.pallas_call(
        gather_kernel,
        out_shape=pltpu.VMEM((rows, width), jnp.bfloat16),
        in_specs=[pl.BlockSpec(memory_space=pltpu.SMEM)] + [pl.BlockSpec(memory_space=pl.ANY)] * len(pieces),
        out_specs=pl.BlockSpec(memory_space=pltpu.VMEM),
        scratch_shapes=[pltpu.SemaphoreType.DMA((len(pieces),))],
        compiler_params=pltpu.CompilerParams(vmem_limit_bytes=VMEM_LIMIT),
        cost_estimate=pl.CostEstimate(flops=0, bytes_accessed=4 * rows * width, transcendentals=0),
    )(spot, *pieces)


def project_kernel(planes, at, spot, a_ref, *refs):
    blocks, (here, there, w_ref, acc, sems) = refs[:12], refs[12:]
    tile = a_ref.shape[0] // 2
    cols = w_ref.shape[1]
    shard = w_ref.shape[0] // (planes * GW)
    block = GW * shard
    plane, core = spot[2], spot[3]
    last = planes - 1

    def copies(i, source):
        for j in range(2):
            side = core if j == 0 else 1 - core
            for x in range(2):
                src = blocks[2 * i + j].at[pl.ds(x * shard, shard), pl.ds(at, cols)]
                row = pl.multiple_of(source * block + (2 * x + side) * shard, shard)
                yield pltpu.make_async_copy(src, w_ref.at[pl.ds(row, shard), :], sems.at[4 * i + 2 * j + x])

    middle = (plane > 0) & (plane < last)
    wanted = (
        (0, plane, None),
        (1, plane - 1, plane > 0),
        (2, plane + 1, plane < last),
        (3, jnp.where(plane == 1, 3, 0), middle),
        (4, jnp.where(plane == 0, 2, 1), jnp.logical_not(middle)),
        (5, last - plane, jnp.logical_not(middle)),
    )

    def each(act):
        for i, source, when in wanted:
            if when is None:
                for c in copies(i, source):
                    act(c)
            else:

                @pl.when(when)
                def _():
                    for c in copies(i, source):
                        act(c)

    each(lambda c: c.start())
    each(lambda c: c.wait())
    acc[...] = jnp.dot(a_ref[...], w_ref[...], preferred_element_type=jnp.float32)
    here[...] = acc[:tile, :].astype(jnp.bfloat16)
    there[...] = acc[tile:, :].astype(jnp.bfloat16)


def project(spot, a, blocks, at, cols, planes):
    rows, deep = a.shape
    vmem, hbm = pl.BlockSpec(memory_space=pltpu.VMEM), pl.BlockSpec(memory_space=pltpu.HBM)
    return pl.pallas_call(
        functools.partial(project_kernel, planes, at),
        out_shape=[jax.ShapeDtypeStruct((rows // 2, cols), jnp.bfloat16)] * 2,
        in_specs=[pl.BlockSpec(memory_space=pltpu.SMEM), vmem] + [hbm] * len(blocks),
        out_specs=[vmem] * 2,
        scratch_shapes=[
            pltpu.VMEM((deep, cols), jnp.bfloat16),
            pltpu.VMEM((rows, cols), jnp.float32),
            pltpu.SemaphoreType.DMA((24,)),
        ],
        compiler_params=pltpu.CompilerParams(vmem_limit_bytes=VMEM_LIMIT // 4),
        cost_estimate=pl.CostEstimate(
            flops=2 * rows * deep * cols,
            bytes_accessed=2 * (rows * deep + deep * cols + rows * cols),
            transcendentals=0,
        ),
    )(spot, a, *blocks)


def local_plane(queries, keys, values, window, out_weight):
    span = lax.axis_size("seq")
    planes = span // GW
    down = [(i, i + GW) for i in range(span - GW)]
    up = [(i + GW, i) for i in range(span - GW)]
    mates = [(i, i ^ 1) for i in range(span)]
    outer = [(i, i ^ 3) for i in range(span) if i % GW in (1, 2)]
    partners = [(i, i ^ 2) for i in range(span)]
    seq, side = lax.axis_index("seq"), lax.axis_index("head")
    half = seq // 2 % 2
    tile, own_width = keys.shape
    heads = own_width // HEAD_DIM

    def move(array, pairs):
        return lax.ppermute(array, "seq", pairs)

    def in_order(flag, own, other, axis):
        return jnp.where(
            flag == 0, jnp.concatenate([own, other], axis=axis), jnp.concatenate([other, own], axis=axis)
        )

    def line(array):
        return [array, move(array, mates), move(array, outer)]

    kv = jnp.concatenate([keys, values], axis=0)
    kv_up, kv_dn = move(kv, down), move(kv, up)
    q_own = lax.dynamic_slice_in_dim(queries, side * own_width, own_width, 1)
    q_else = lax.dynamic_slice_in_dim(queries, (1 - side) * own_width, own_width, 1)
    q = in_order(side, q_own, lax.ppermute(q_else, "head", [(0, 1), (1, 0)]), 0)

    cols = out_weight.shape[1] // 2
    w_mine = lax.dynamic_slice_in_dim(out_weight, half * cols, cols, 1)
    w_theirs = move(lax.dynamic_slice_in_dim(out_weight, (1 - half) * cols, cols, 1), partners)
    w_own = in_order(half, w_mine, w_theirs, 0)

    kv, w_own = lax.optimization_barrier((kv, w_own))
    own = line(kv)

    kv_up, kv_dn, own, q, w_own = lax.optimization_barrier((kv_up, kv_dn, own, q, w_own))
    plane = seq // GW
    w_up, w_dn = move(w_own, down), move(w_own, up)
    w_mate = move(w_own, mates)

    part = heads // 3
    cuts = [0, 2 * part * HEAD_DIM, own_width]
    rows = [
        line(jnp.concatenate([kv_up[:, lo:hi], kv_dn[:, lo:hi]], axis=0)) for lo, hi in zip(cuts[:-1], cuts[1:])
    ]

    def between(*pairs):
        return [(a * GW + c, b * GW + c) for a, b in pairs for c in range(GW)]

    w_own, w_up, w_dn = lax.optimization_barrier((w_own, w_up, w_dn))
    blocks = [w_own, w_mate, w_up, move(w_up, mates), w_dn, move(w_dn, mates)]
    for far in (
        move(w_own, between((0, 2), (3, 1))),
        move(jnp.where(plane == planes - 2, w_up, w_dn), between((2, 3), (1, 0))),
        move(w_own, between((0, 3), (3, 0))),
    ):
        blocks += [far, move(far, mates)]

    listed = jnp.concatenate([window[0], seq[None]])
    pieces = []
    for n, (held, first) in enumerate(((0, 0), (0, part), (1, 0))):
        mine = attend_tile(listed, q, n * part, part, first, own, rows[held], pieces[1:2] if n == 2 else [])
        pieces += [
            mine,
            move(mine, partners),
            lax.ppermute(mine, "head", [(0, 1), (1, 0)]),
            lax.ppermute(mine, ("seq", "head"), [(2 * i + y, 2 * (i ^ 2) + 1 - y) for i in range(span) for y in (0, 1)]),
        ]

    spot = jnp.stack([side, half, plane, seq % 2])
    made, sent = [], []
    third = cols // 3
    attended = gather_heads(spot, pieces)
    for at in range(0, cols, third):
        here, there = project(spot, attended, blocks, at, third, planes)
        made.append(here)
        sent.append(move(there, partners))
    return in_order(half, jnp.concatenate(made, axis=1), jnp.concatenate(sent, axis=1), 1)


def solution(mesh):
    span, sides = mesh.shape["seq"], mesh.shape["head"]

    def local(queries, keys, values, window, out_weight):
        one_step = span == GH * GW and sides == 2
        even = keys.shape[1] % (3 * HEAD_DIM) == 0 and out_weight.shape[1] % 1536 == 0
        which = local_plane if one_step and even else local_general
        return which(queries, keys, values, window, out_weight)

    in_specs = (
        P(("seq", "head"), None),
        P("seq", "head"),
        P("seq", "head"),
        P("seq", None),
        P("seq", "head"),
    )
    out_specs = P("seq", "head")
    return jax.shard_map(local, mesh=mesh, in_specs=in_specs, out_specs=out_specs, check_vma=False)
```

```python
import functools

import jax
import jax.numpy as jnp
from jax import lax
from jax.experimental import pallas as pl
from jax.experimental.pallas import tpu as pltpu
from jax.sharding import PartitionSpec as P

HEAD_DIM = 128
GH = 4
GW = 4
LOG2E = 1.4426950408889634
DEAD = -1e30


def passed_along(array, axis, by):
    count = lax.axis_size(axis)
    pairs = [(i, i + by) for i in range(count) if 0 <= i + by < count]
    return lax.ppermute(array, axis, pairs)


def attend_block(softmax_state, queries, kv_block, live_keys):
    run_max, run_sum, run_acc = softmax_state
    factor = queries.shape[-1] ** (-0.5)
    scores = (
        jnp.einsum("qhd,khd->qhk", queries, kv_block[0], preferred_element_type=jnp.float32)
        * factor
    )
    scores = jnp.where(live_keys[None, None, :], scores, -1e30)
    new_max = jnp.maximum(run_max, jnp.max(scores, axis=-1))
    rescale = jnp.exp(run_max - new_max)
    weights = jnp.where(live_keys[None, None, :], jnp.exp(scores - new_max[:, :, None]), 0.0)
    run_sum = run_sum * rescale + jnp.sum(weights, axis=-1)
    run_acc = run_acc * rescale[:, :, None] + jnp.einsum(
        "qhk,khd->qhd",
        weights.astype(jnp.bfloat16),
        kv_block[1],
        preferred_element_type=jnp.float32,
    )
    return (new_max, run_sum, run_acc)


def local_general(queries, keys, values, window, out_weight):
    tok_rows = queries.shape[0]
    head_width = HEAD_DIM
    heads_all = queries.shape[1] // head_width
    local_q = lax.all_to_all(
        queries.reshape(tok_rows, heads_all, head_width),
        "head",
        split_axis=1,
        concat_axis=0,
        tiled=True,
    )
    tile_rows = local_q.shape[0]
    heads_dev = local_q.shape[1]
    live_tiles = window[0] >= 0
    kv_pair = jnp.stack(
        [
            keys.reshape(tile_rows, heads_dev, head_width),
            values.reshape(tile_rows, heads_dev, head_width),
        ]
    )
    softmax_state = (
        jnp.full((tile_rows, heads_dev), -1e30, jnp.float32),
        jnp.zeros((tile_rows, heads_dev), jnp.float32),
        jnp.zeros((tile_rows, heads_dev, head_width), jnp.float32),
    )
    seq_span = lax.axis_size("seq")
    plane_size = GH * GW

    def tile_mask(first_slot, tile_count):
        return jnp.repeat(live_tiles[first_slot : first_slot + tile_count], tile_rows)

    from_left = passed_along(kv_pair, "seq", 1)
    from_right = passed_along(kv_pair, "seq", -1)
    kv_line = jnp.concatenate([from_left, kv_pair, from_right], axis=1)
    above = passed_along(kv_line, "seq", GW)
    below = passed_along(kv_line, "seq", -GW)
    kv_plane = jnp.concatenate([above, kv_line, below], axis=1)
    line_rows = 3 * tile_rows
    for row_index in (1, 0, 2):
        softmax_state = attend_block(
            softmax_state,
            local_q,
            kv_plane[:, row_index * line_rows : (row_index + 1) * line_rows],
            tile_mask(9 + 3 * row_index, 3),
        )
    if plane_size < seq_span:
        for depth_step in (-1, 1):
            kv_depth = passed_along(kv_plane, "seq", -depth_step * plane_size)
            for row_index in range(3):
                softmax_state = attend_block(
                    softmax_state,
                    local_q,
                    kv_depth[:, row_index * line_rows : (row_index + 1) * line_rows],
                    tile_mask(9 * (depth_step + 1) + 3 * row_index, 3),
                )
    run_max, run_sum, run_acc = softmax_state
    finished = (run_acc / run_sum[:, :, None]).astype(jnp.bfloat16)
    finished = finished.reshape(tile_rows, heads_dev * head_width)
    all_heads = lax.all_gather(finished, "head", axis=1, tiled=True)
    projected = jnp.dot(
        all_heads,
        lax.all_gather(out_weight, "seq", axis=0, tiled=True),
        preferred_element_type=jnp.float32,
    )
    return projected.astype(jnp.bfloat16)


VMEM_LIMIT = 56 * 2**20


def attend_kernel(listed, q_ref, *refs):
    o_ref = refs[-1]
    keys, values = refs[:9], refs[9:18]
    coef = HEAD_DIM**-0.5 * LOG2E
    toward = 1 - 2 * (listed[27] & 1)
    for head in range(q_ref.shape[1] // HEAD_DIM):
        at = slice(head * HEAD_DIM, (head + 1) * HEAD_DIM)
        q = q_ref[:, at]
        top = total = acc = None
        for r in (1, 0, 2):
            scores, lives = [], []
            new = top
            for k, step in enumerate((0, toward, -toward)):
                s = lax.dot_general(
                    keys[3 * r + k][:, at], q, (((1,), (1,)), ((), ())), preferred_element_type=jnp.float32
                )
                live = listed[10 + 3 * r + step] >= 0
                scores.append(s)
                lives.append(live)
                high = jnp.where(live, jnp.max(s, axis=0, keepdims=True), DEAD)
                new = high if new is None else jnp.maximum(new, high)
            weights, part = [], None
            for s, live in zip(scores, lives):
                w = jnp.exp2((s - jnp.where(live, new, -DEAD)) * coef)
                w_sum = jnp.sum(w, axis=0, keepdims=True)
                part = w_sum if part is None else part + w_sum
                weights.append(w.astype(jnp.bfloat16))
            sides = jnp.concatenate([values[3 * r + k][:, at].T for k in range(3)], axis=1)
            pv = jnp.dot(sides, jnp.concatenate(weights, axis=0), preferred_element_type=jnp.float32)
            if top is None:
                total, acc = part, pv
            else:
                again = jnp.exp2((top - new) * coef)
                total = total * again + part
                acc = acc * again + pv
            top = new
        o_ref[:, at] = (acc / total).astype(jnp.bfloat16).T


AT_ONCE = 2


def attend_tile(listed, q, head, count, first, own, rows, before):
    tile = q.shape[0]

    def spec(block, at=first):
        return pl.BlockSpec((tile, AT_ONCE * HEAD_DIM), lambda h, listed: (block, at // AT_ONCE + h))

    return pl.pallas_call(
        attend_kernel,
        out_shape=jax.ShapeDtypeStruct((tile, count * HEAD_DIM), jnp.bfloat16),
        grid_spec=pltpu.PrefetchScalarGridSpec(
            num_scalar_prefetch=1,
            grid=(count // AT_ONCE,),
            in_specs=[spec(0, head)]
            + [spec(0)] * 3
            + [spec(0, head)] * 3
            + [spec(2)] * 3
            + [spec(1)] * 3
            + [spec(1, head)] * 3
            + [spec(3)] * 3
            + [pl.BlockSpec(memory_space=pl.ANY)] * len(before),
            out_specs=pl.BlockSpec((tile, AT_ONCE * HEAD_DIM), lambda h, listed: (0, h)),
        ),
        compiler_params=pltpu.CompilerParams(vmem_limit_bytes=VMEM_LIMIT),
        cost_estimate=pl.CostEstimate(flops=1, bytes_accessed=1, transcendentals=0),
    )(listed, q, *rows, *own, *rows, *rows, *own, *rows, *before)


def gather_kernel(spot, *refs):
    pieces, a_ref, sems = refs[:-2], refs[-2], refs[-1]
    tile = a_ref.shape[0] // 2
    side_width = a_ref.shape[1] // 2
    copies, at = [], 0
    for i, piece in enumerate(pieces):
        wide = piece.shape[1]
        col = (spot[0] if i % 4 < 2 else 1 - spot[0]) * side_width + at
        dst = a_ref.at[pl.ds(i % 2 * tile, tile), pl.ds(pl.multiple_of(col, 128), wide)]
        copies.append(pltpu.make_async_copy(piece, dst, sems.at[i]))
        at += wide if i % 4 == 3 else 0
    for c in copies:
        c.start()
    for c in copies:
        c.wait()


def gather_heads(spot, pieces):
    rows, width = 2 * pieces[0].shape[0], 2 * sum(p.shape[1] for p in pieces[::4])
    return pl.pallas_call(
        gather_kernel,
        out_shape=pltpu.VMEM((rows, width), jnp.bfloat16),
        in_specs=[pl.BlockSpec(memory_space=pltpu.SMEM)] + [pl.BlockSpec(memory_space=pl.ANY)] * len(pieces),
        out_specs=pl.BlockSpec(memory_space=pltpu.VMEM),
        scratch_shapes=[pltpu.SemaphoreType.DMA((len(pieces),))],
        compiler_params=pltpu.CompilerParams(vmem_limit_bytes=VMEM_LIMIT),
        cost_estimate=pl.CostEstimate(flops=0, bytes_accessed=4 * rows * width, transcendentals=0),
    )(spot, *pieces)


def project_kernel(planes, at, spot, a_ref, *refs):
    blocks, (here, there, w_ref, acc, sems) = refs[:12], refs[12:]
    tile = a_ref.shape[0] // 2
    cols = w_ref.shape[1]
    shard = w_ref.shape[0] // (planes * GW)
    block = GW * shard
    plane, core = spot[2], spot[3]
    last = planes - 1

    def copies(i, source):
        for j in range(2):
            side = core if j == 0 else 1 - core
            for x in range(2):
                src = blocks[2 * i + j].at[pl.ds(x * shard, shard), pl.ds(at, cols)]
                row = pl.multiple_of(source * block + (2 * x + side) * shard, shard)
                yield pltpu.make_async_copy(src, w_ref.at[pl.ds(row, shard), :], sems.at[4 * i + 2 * j + x])

    middle = (plane > 0) & (plane < last)
    wanted = (
        (0, plane, None),
        (1, plane - 1, plane > 0),
        (2, plane + 1, plane < last),
        (3, jnp.where(plane == 1, 3, 0), middle),
        (4, jnp.where(plane == 0, 2, 1), jnp.logical_not(middle)),
        (5, last - plane, jnp.logical_not(middle)),
    )

    def each(act):
        for i, source, when in wanted:
            if when is None:
                for c in copies(i, source):
                    act(c)
            else:

                @pl.when(when)
                def _():
                    for c in copies(i, source):
                        act(c)

    each(lambda c: c.start())
    each(lambda c: c.wait())
    acc[...] = jnp.dot(a_ref[...], w_ref[...], preferred_element_type=jnp.float32)
    here[...] = acc[:tile, :].astype(jnp.bfloat16)
    there[...] = acc[tile:, :].astype(jnp.bfloat16)


def project(spot, a, blocks, at, cols, planes):
    rows, deep = a.shape
    vmem, hbm = pl.BlockSpec(memory_space=pltpu.VMEM), pl.BlockSpec(memory_space=pltpu.HBM)
    return pl.pallas_call(
        functools.partial(project_kernel, planes, at),
        out_shape=[jax.ShapeDtypeStruct((rows // 2, cols), jnp.bfloat16)] * 2,
        in_specs=[pl.BlockSpec(memory_space=pltpu.SMEM), vmem] + [hbm] * len(blocks),
        out_specs=[vmem] * 2,
        scratch_shapes=[
            pltpu.VMEM((deep, cols), jnp.bfloat16),
            pltpu.VMEM((rows, cols), jnp.float32),
            pltpu.SemaphoreType.DMA((24,)),
        ],
        compiler_params=pltpu.CompilerParams(vmem_limit_bytes=VMEM_LIMIT // 4),
        cost_estimate=pl.CostEstimate(
            flops=2 * rows * deep * cols,
            bytes_accessed=2 * (rows * deep + deep * cols + rows * cols),
            transcendentals=0,
        ),
    )(spot, a, *blocks)


def local_plane(queries, keys, values, window, out_weight):
    span = lax.axis_size("seq")
    planes = span // GW
    down = [(i, i + GW) for i in range(span - GW)]
    up = [(i + GW, i) for i in range(span - GW)]
    mates = [(i, i ^ 1) for i in range(span)]
    outer = [(i, i ^ 3) for i in range(span) if i % GW in (1, 2)]
    partners = [(i, i ^ 2) for i in range(span)]
    seq, side = lax.axis_index("seq"), lax.axis_index("head")
    half = seq // 2 % 2
    tile, own_width = keys.shape
    heads = own_width // HEAD_DIM

    def move(array, pairs):
        return lax.ppermute(array, "seq", pairs)

    def in_order(flag, own, other, axis):
        return jnp.where(
            flag == 0, jnp.concatenate([own, other], axis=axis), jnp.concatenate([other, own], axis=axis)
        )

    def line(array):
        return [array, move(array, mates), move(array, outer)]

    kv = jnp.concatenate([keys, values], axis=0)
    kv_up, kv_dn = move(kv, down), move(kv, up)
    q_own = lax.dynamic_slice_in_dim(queries, side * own_width, own_width, 1)
    q_else = lax.dynamic_slice_in_dim(queries, (1 - side) * own_width, own_width, 1)
    q = in_order(side, q_own, lax.ppermute(q_else, "head", [(0, 1), (1, 0)]), 0)

    cols = out_weight.shape[1] // 2
    w_mine = lax.dynamic_slice_in_dim(out_weight, half * cols, cols, 1)
    w_theirs = move(lax.dynamic_slice_in_dim(out_weight, (1 - half) * cols, cols, 1), partners)
    w_own = in_order(half, w_mine, w_theirs, 0)

    kv, w_own = lax.optimization_barrier((kv, w_own))
    own = line(kv)

    kv_up, kv_dn, own, q, w_own = lax.optimization_barrier((kv_up, kv_dn, own, q, w_own))
    plane = seq // GW
    w_up, w_dn = move(w_own, down), move(w_own, up)
    w_mate = move(w_own, mates)

    part = heads // 3
    cuts = [0, 2 * part * HEAD_DIM, own_width]
    rows = [
        line(jnp.concatenate([kv_up[:, lo:hi], kv_dn[:, lo:hi]], axis=0)) for lo, hi in zip(cuts[:-1], cuts[1:])
    ]

    def between(*pairs):
        return [(a * GW + c, b * GW + c) for a, b in pairs for c in range(GW)]

    w_own, w_up, w_dn = lax.optimization_barrier((w_own, w_up, w_dn))
    blocks = [w_own, w_mate, w_up, move(w_up, mates), w_dn, move(w_dn, mates)]
    passed = move(jnp.where(plane == planes - 2, w_up, w_dn), between((2, 3), (1, 0)))
    ends = move(w_own, between((0, 3), (3, 0)))
    for far in (move(w_own, between((0, 2), (3, 1))), passed, ends):
        blocks += [far, move(far, mates)]

    listed = jnp.concatenate([window[0], seq[None]])
    pieces = []
    for n, (held, first) in enumerate(((0, 0), (0, part), (1, 0))):
        mine = attend_tile(listed, q, n * part, part, first, own, rows[held], pieces[1:2] if n == 2 else [])
        pieces += [
            mine,
            move(mine, partners),
            lax.ppermute(mine, "head", [(0, 1), (1, 0)]),
            lax.ppermute(mine, ("seq", "head"), [(2 * i + y, 2 * (i ^ 2) + 1 - y) for i in range(span) for y in (0, 1)]),
        ]

    spot = jnp.stack([side, half, plane, seq % 2])
    made, sent = [], []
    third = cols // 3
    attended = gather_heads(spot, pieces)
    for at in range(0, cols, third):
        here, there = project(spot, attended, blocks, at, third, planes)
        made.append(here)
        sent.append(move(there, partners))
    return in_order(half, jnp.concatenate(made, axis=1), jnp.concatenate(sent, axis=1), 1)


def solution(mesh):
    span, sides = mesh.shape["seq"], mesh.shape["head"]

    def local(queries, keys, values, window, out_weight):
        one_step = span == GH * GW and sides == 2
        even = keys.shape[1] % (3 * HEAD_DIM) == 0 and out_weight.shape[1] % 1536 == 0
        which = local_plane if one_step and even else local_general
        return which(queries, keys, values, window, out_weight)

    in_specs = (
        P(("seq", "head"), None),
        P("seq", "head"),
        P("seq", "head"),
        P("seq", None),
        P("seq", "head"),
    )
    out_specs = P("seq", "head")
    return jax.shard_map(local, mesh=mesh, in_specs=in_specs, out_specs=out_specs, check_vma=False)
```

```python
import functools

import jax
import jax.numpy as jnp
from jax import lax
from jax.experimental import pallas as pl
from jax.experimental.pallas import tpu as pltpu
from jax.sharding import PartitionSpec as P

HEAD_DIM = 128
GH = 4
GW = 4
LOG2E = 1.4426950408889634
DEAD = -1e30


def passed_along(array, axis, by):
    count = lax.axis_size(axis)
    pairs = [(i, i + by) for i in range(count) if 0 <= i + by < count]
    return lax.ppermute(array, axis, pairs)


def attend_block(softmax_state, queries, kv_block, live_keys):
    run_max, run_sum, run_acc = softmax_state
    factor = queries.shape[-1] ** (-0.5)
    scores = (
        jnp.einsum("qhd,khd->qhk", queries, kv_block[0], preferred_element_type=jnp.float32)
        * factor
    )
    scores = jnp.where(live_keys[None, None, :], scores, -1e30)
    new_max = jnp.maximum(run_max, jnp.max(scores, axis=-1))
    rescale = jnp.exp(run_max - new_max)
    weights = jnp.where(live_keys[None, None, :], jnp.exp(scores - new_max[:, :, None]), 0.0)
    run_sum = run_sum * rescale + jnp.sum(weights, axis=-1)
    run_acc = run_acc * rescale[:, :, None] + jnp.einsum(
        "qhk,khd->qhd",
        weights.astype(jnp.bfloat16),
        kv_block[1],
        preferred_element_type=jnp.float32,
    )
    return (new_max, run_sum, run_acc)


def local_general(queries, keys, values, window, out_weight):
    tok_rows = queries.shape[0]
    head_width = HEAD_DIM
    heads_all = queries.shape[1] // head_width
    local_q = lax.all_to_all(
        queries.reshape(tok_rows, heads_all, head_width),
        "head",
        split_axis=1,
        concat_axis=0,
        tiled=True,
    )
    tile_rows = local_q.shape[0]
    heads_dev = local_q.shape[1]
    live_tiles = window[0] >= 0
    kv_pair = jnp.stack(
        [
            keys.reshape(tile_rows, heads_dev, head_width),
            values.reshape(tile_rows, heads_dev, head_width),
        ]
    )
    softmax_state = (
        jnp.full((tile_rows, heads_dev), -1e30, jnp.float32),
        jnp.zeros((tile_rows, heads_dev), jnp.float32),
        jnp.zeros((tile_rows, heads_dev, head_width), jnp.float32),
    )
    seq_span = lax.axis_size("seq")
    plane_size = GH * GW

    def tile_mask(first_slot, tile_count):
        return jnp.repeat(live_tiles[first_slot : first_slot + tile_count], tile_rows)

    from_left = passed_along(kv_pair, "seq", 1)
    from_right = passed_along(kv_pair, "seq", -1)
    kv_line = jnp.concatenate([from_left, kv_pair, from_right], axis=1)
    above = passed_along(kv_line, "seq", GW)
    below = passed_along(kv_line, "seq", -GW)
    kv_plane = jnp.concatenate([above, kv_line, below], axis=1)
    line_rows = 3 * tile_rows
    for row_index in (1, 0, 2):
        softmax_state = attend_block(
            softmax_state,
            local_q,
            kv_plane[:, row_index * line_rows : (row_index + 1) * line_rows],
            tile_mask(9 + 3 * row_index, 3),
        )
    if plane_size < seq_span:
        for depth_step in (-1, 1):
            kv_depth = passed_along(kv_plane, "seq", -depth_step * plane_size)
            for row_index in range(3):
                softmax_state = attend_block(
                    softmax_state,
                    local_q,
                    kv_depth[:, row_index * line_rows : (row_index + 1) * line_rows],
                    tile_mask(9 * (depth_step + 1) + 3 * row_index, 3),
                )
    run_max, run_sum, run_acc = softmax_state
    finished = (run_acc / run_sum[:, :, None]).astype(jnp.bfloat16)
    finished = finished.reshape(tile_rows, heads_dev * head_width)
    all_heads = lax.all_gather(finished, "head", axis=1, tiled=True)
    projected = jnp.dot(
        all_heads,
        lax.all_gather(out_weight, "seq", axis=0, tiled=True),
        preferred_element_type=jnp.float32,
    )
    return projected.astype(jnp.bfloat16)


VMEM_LIMIT = 56 * 2**20


def attend_kernel(listed, q_ref, *refs):
    o_ref = refs[-1]
    tiles = refs[:9]
    tile = q_ref.shape[0]
    coef = HEAD_DIM**-0.5 * LOG2E
    toward = 1 - 2 * (listed[27] & 1)
    for head in range(q_ref.shape[1] // HEAD_DIM):
        at = slice(head * HEAD_DIM, (head + 1) * HEAD_DIM)
        q = q_ref[:, at]
        top = total = acc = None
        for r in (1, 0, 2):
            scores, lives = [], []
            new = top
            for k, step in enumerate((0, toward, -toward)):
                s = lax.dot_general(
                    tiles[3 * r + k][:tile, at], q, (((1,), (1,)), ((), ())), preferred_element_type=jnp.float32
                )
                live = listed[10 + 3 * r + step] >= 0
                scores.append(s)
                lives.append(live)
                high = jnp.where(live, jnp.max(s, axis=0, keepdims=True), DEAD)
                new = high if new is None else jnp.maximum(new, high)
            weights, part = [], None
            for s, live in zip(scores, lives):
                w = jnp.exp2((s - jnp.where(live, new, -DEAD)) * coef)
                w_sum = jnp.sum(w, axis=0, keepdims=True)
                part = w_sum if part is None else part + w_sum
                weights.append(w.astype(jnp.bfloat16))
            sides = jnp.concatenate([tiles[3 * r + k][tile:, at].T for k in range(3)], axis=1)
            pv = jnp.dot(sides, jnp.concatenate(weights, axis=0), preferred_element_type=jnp.float32)
            if top is None:
                total, acc = part, pv
            else:
                again = jnp.exp2((top - new) * coef)
                total = total * again + part
                acc = acc * again + pv
            top = new
        o_ref[:, at] = (acc / total).astype(jnp.bfloat16).T


AT_ONCE = 2


def attend_tile(listed, q, head, count, first, own, rows, before):
    tile = q.shape[0]

    def spec(block, at=first, rows=2 * tile):
        return pl.BlockSpec((rows, AT_ONCE * HEAD_DIM), lambda h, listed: (block, at // AT_ONCE + h))

    return pl.pallas_call(
        attend_kernel,
        out_shape=jax.ShapeDtypeStruct((tile, count * HEAD_DIM), jnp.bfloat16),
        grid_spec=pltpu.PrefetchScalarGridSpec(
            num_scalar_prefetch=1,
            grid=(count // AT_ONCE,),
            in_specs=[spec(0, head, tile)]
            + [spec(0)] * 3
            + [spec(0, head)] * 3
            + [spec(1)] * 3
            + [pl.BlockSpec(memory_space=pl.ANY)] * len(before),
            out_specs=pl.BlockSpec((tile, AT_ONCE * HEAD_DIM), lambda h, listed: (0, h)),
        ),
        compiler_params=pltpu.CompilerParams(vmem_limit_bytes=VMEM_LIMIT),
        cost_estimate=pl.CostEstimate(flops=1, bytes_accessed=1, transcendentals=0),
    )(listed, q, *rows, *own, *rows, *before)


def gather_kernel(spot, *refs):
    pieces, a_ref, sems = refs[:-2], refs[-2], refs[-1]
    tile = a_ref.shape[0] // 2
    side_width = a_ref.shape[1] // 2
    copies, at = [], 0
    for i, piece in enumerate(pieces):
        wide = piece.shape[1]
        col = (spot[0] if i % 4 < 2 else 1 - spot[0]) * side_width + at
        dst = a_ref.at[pl.ds(i % 2 * tile, tile), pl.ds(pl.multiple_of(col, 128), wide)]
        copies.append(pltpu.make_async_copy(piece, dst, sems.at[i]))
        at += wide if i % 4 == 3 else 0
    for c in copies:
        c.start()
    for c in copies:
        c.wait()


def gather_heads(spot, pieces):
    rows, width = 2 * pieces[0].shape[0], 2 * sum(p.shape[1] for p in pieces[::4])
    return pl.pallas_call(
        gather_kernel,
        out_shape=pltpu.VMEM((rows, width), jnp.bfloat16),
        in_specs=[pl.BlockSpec(memory_space=pltpu.SMEM)] + [pl.BlockSpec(memory_space=pl.ANY)] * len(pieces),
        out_specs=pl.BlockSpec(memory_space=pltpu.VMEM),
        scratch_shapes=[pltpu.SemaphoreType.DMA((len(pieces),))],
        compiler_params=pltpu.CompilerParams(vmem_limit_bytes=VMEM_LIMIT),
        cost_estimate=pl.CostEstimate(flops=0, bytes_accessed=4 * rows * width, transcendentals=0),
    )(spot, *pieces)


def project_kernel(planes, at, spot, a_ref, *refs):
    blocks, (here, there, w_ref, acc, sems) = refs[:12], refs[12:]
    tile = a_ref.shape[0] // 2
    cols = w_ref.shape[1]
    shard = w_ref.shape[0] // (planes * GW)
    block = GW * shard
    plane, core = spot[2], spot[3]
    last = planes - 1

    def copies(i, source):
        for j in range(2):
            side = core if j == 0 else 1 - core
            for x in range(2):
                src = blocks[2 * i + j].at[pl.ds(x * shard, shard), pl.ds(at, cols)]
                row = pl.multiple_of(source * block + (2 * x + side) * shard, shard)
                yield pltpu.make_async_copy(src, w_ref.at[pl.ds(row, shard), :], sems.at[4 * i + 2 * j + x])

    middle = (plane > 0) & (plane < last)
    wanted = (
        (0, plane, None),
        (1, plane - 1, plane > 0),
        (2, plane + 1, plane < last),
        (3, jnp.where(plane == 1, 3, 0), middle),
        (4, jnp.where(plane == 0, 2, 1), jnp.logical_not(middle)),
        (5, last - plane, jnp.logical_not(middle)),
    )

    def each(act):
        for i, source, when in wanted:
            if when is None:
                for c in copies(i, source):
                    act(c)
            else:

                @pl.when(when)
                def _():
                    for c in copies(i, source):
                        act(c)

    each(lambda c: c.start())
    each(lambda c: c.wait())
    acc[...] = jnp.dot(a_ref[...], w_ref[...], preferred_element_type=jnp.float32)
    here[...] = acc[:tile, :].astype(jnp.bfloat16)
    there[...] = acc[tile:, :].astype(jnp.bfloat16)


def project(spot, a, blocks, at, cols, planes):
    rows, deep = a.shape
    vmem, hbm = pl.BlockSpec(memory_space=pltpu.VMEM), pl.BlockSpec(memory_space=pltpu.HBM)
    return pl.pallas_call(
        functools.partial(project_kernel, planes, at),
        out_shape=[jax.ShapeDtypeStruct((rows // 2, cols), jnp.bfloat16)] * 2,
        in_specs=[pl.BlockSpec(memory_space=pltpu.SMEM), vmem] + [hbm] * len(blocks),
        out_specs=[vmem] * 2,
        scratch_shapes=[
            pltpu.VMEM((deep, cols), jnp.bfloat16),
            pltpu.VMEM((rows, cols), jnp.float32),
            pltpu.SemaphoreType.DMA((24,)),
        ],
        compiler_params=pltpu.CompilerParams(vmem_limit_bytes=VMEM_LIMIT // 4),
        cost_estimate=pl.CostEstimate(
            flops=2 * rows * deep * cols,
            bytes_accessed=2 * (rows * deep + deep * cols + rows * cols),
            transcendentals=0,
        ),
    )(spot, a, *blocks)


def local_plane(queries, keys, values, window, out_weight):
    span = lax.axis_size("seq")
    planes = span // GW
    down = [(i, i + GW) for i in range(span - GW)]
    up = [(i + GW, i) for i in range(span - GW)]
    mates = [(i, i ^ 1) for i in range(span)]
    outer = [(i, i ^ 3) for i in range(span) if i % GW in (1, 2)]
    partners = [(i, i ^ 2) for i in range(span)]
    seq, side = lax.axis_index("seq"), lax.axis_index("head")
    half = seq // 2 % 2
    tile, own_width = keys.shape
    heads = own_width // HEAD_DIM

    def move(array, pairs):
        return lax.ppermute(array, "seq", pairs)

    def in_order(flag, own, other, axis):
        return jnp.where(
            flag == 0, jnp.concatenate([own, other], axis=axis), jnp.concatenate([other, own], axis=axis)
        )

    def line(array):
        return [array, move(array, mates), move(array, outer)]

    kv = jnp.concatenate([keys, values], axis=0)
    kv_up, kv_dn = move(kv, down), move(kv, up)
    q_own = lax.dynamic_slice_in_dim(queries, side * own_width, own_width, 1)
    q_else = lax.dynamic_slice_in_dim(queries, (1 - side) * own_width, own_width, 1)
    q = in_order(side, q_own, lax.ppermute(q_else, "head", [(0, 1), (1, 0)]), 0)

    cols = out_weight.shape[1] // 2
    w_mine = lax.dynamic_slice_in_dim(out_weight, half * cols, cols, 1)
    w_theirs = move(lax.dynamic_slice_in_dim(out_weight, (1 - half) * cols, cols, 1), partners)
    w_own = in_order(half, w_mine, w_theirs, 0)

    kv, w_own = lax.optimization_barrier((kv, w_own))
    own = line(kv)

    kv_up, kv_dn, own, q, w_own = lax.optimization_barrier((kv_up, kv_dn, own, q, w_own))
    plane = seq // GW
    w_up, w_dn = move(w_own, down), move(w_own, up)
    w_mate = move(w_own, mates)

    part = heads // 3
    cuts = [0, 2 * part * HEAD_DIM, own_width]
    rows = [
        line(jnp.concatenate([kv_up[:, lo:hi], kv_dn[:, lo:hi]], axis=0)) for lo, hi in zip(cuts[:-1], cuts[1:])
    ]

    def between(*pairs):
        return [(a * GW + c, b * GW + c) for a, b in pairs for c in range(GW)]

    w_own, w_up, w_dn = lax.optimization_barrier((w_own, w_up, w_dn))
    blocks = [w_own, w_mate, w_up, move(w_up, mates), w_dn, move(w_dn, mates)]
    passed = move(jnp.where(plane == planes - 2, w_up, w_dn), between((2, 3), (1, 0)))
    ends = move(w_own, between((0, 3), (3, 0)))
    for far in (move(w_own, between((0, 2), (3, 1))), passed, ends):
        blocks += [far, move(far, mates)]

    listed = jnp.concatenate([window[0], seq[None]])
    pieces = []
    for n, (held, first) in enumerate(((0, 0), (0, part), (1, 0))):
        mine = attend_tile(listed, q, n * part, part, first, own, rows[held], pieces[1:2] if n == 2 else [])
        pieces += [
            mine,
            move(mine, partners),
            lax.ppermute(mine, "head", [(0, 1), (1, 0)]),
            lax.ppermute(mine, ("seq", "head"), [(2 * i + y, 2 * (i ^ 2) + 1 - y) for i in range(span) for y in (0, 1)]),
        ]

    spot = jnp.stack([side, half, plane, seq % 2])
    made, sent = [], []
    third = cols // 3
    attended = gather_heads(spot, pieces)
    for at in range(0, cols, third):
        here, there = project(spot, attended, blocks, at, third, planes)
        made.append(here)
        sent.append(move(there, partners))
    return in_order(half, jnp.concatenate(made, axis=1), jnp.concatenate(sent, axis=1), 1)


def solution(mesh):
    span, sides = mesh.shape["seq"], mesh.shape["head"]

    def local(queries, keys, values, window, out_weight):
        one_step = span == GH * GW and sides == 2
        even = keys.shape[1] % (3 * HEAD_DIM) == 0 and out_weight.shape[1] % 1536 == 0
        which = local_plane if one_step and even else local_general
        return which(queries, keys, values, window, out_weight)

    in_specs = (
        P(("seq", "head"), None),
        P("seq", "head"),
        P("seq", "head"),
        P("seq", None),
        P("seq", "head"),
    )
    out_specs = P("seq", "head")
    return jax.shard_map(local, mesh=mesh, in_specs=in_specs, out_specs=out_specs, check_vma=False)
```
